128 devices in a mesh: dp: 32 (over z, x, core), sub: 4 (over y).
Axes of the slice: x: 4, y: 4, z: 4, core: 2. Of those that a mesh axis runs over, the one named last changes fastest.
Arguments:
- features: bfloat16 [1048576, 128], P(('dp', 'sub')), may hold values from -6 to 6
- weight_in: bfloat16 [128, 256], replicated, may hold values from -0.5 to 0.5
- bias_in: float32 [256], replicated, may hold values from -3 to 3
- weight_mid: bfloat16 [256, 256], replicated, may hold values from -0.375 to 0.375
- bias_mid: float32 [256], replicated, may hold values from -3 to 3
- weight_out: bfloat16 [256, 172], replicated, may hold values from -0.375 to 0.375
- cotangent: float32 [1048576, 172], P(('dp', 'sub')), may hold values from -6 to 6
- local_tiles: bfloat16 [8192, 4, 128, 128], P(('dp', 'sub')), may hold values from -2 to 2
- local_columns: int32 [8192, 4], P(('dp', 'sub')), may hold values from 0 to 63
- remote_tiles: bfloat16 [8192, 2, 128, 128], P(('dp', 'sub')), may hold values from -2 to 2
- remote_slots: int32 [8192, 2], P(('dp', 'sub')), may hold values from 0 to 15, as said below
- send_rows: int32 [128, 128, 16], P(('dp', 'sub')), may hold values from 0 to 8191, as said below
Outputs:
- weight_in_grad: float32 [128, 256], replicated
- bias_in_grad: float32 [256], replicated
- weight_mid_grad: float32 [256, 256], replicated
- bias_mid_grad: float32 [256], replicated
- weight_out_grad: float32 [256, 172], replicated
- bias_out_grad: float32 [172], replicated
- feature_grad: float32 [1048576, 128], P(('dp', 'sub'))
The draws below stay inside these ranges and needn't reach their ends.
Inputs may be any that keep to these rules, and one draw needn't show every extreme that they name: `remote_slots`: among the tiles of one device every received block number is named at least once. `send_rows`: for each sender and receiver the 16 rows are distinct.
All inputs are finite; a program needn't handle non-finite values.
Results may differ from the reference program's by a relative error of at most 0.0076.
Values may be sent and summed in bfloat16 or wider, within the bound.
A program may use at most 256 MiB of HBM per device.

```python
import jax
import jax.numpy as jnp
from jax import lax

FEAT = 128
HID = 256
CLASSES = 172
BLK = 128
NB = 64
LPB = 4
RPB = 2
SR = 16
STEPS = 3
ROWS = 8192
NODES = 1048576
NBLK = 8192
NRB = 16
N_DP = 32
N_SUB = 4


def tile_values(key, count, width):
    keys = jax.random.split(key, 4)
    shape = (count, width, BLK, BLK)
    keep = jax.random.uniform(keys[0], shape, jnp.float32) < 0.125
    entry = jax.random.uniform(keys[1], shape, jnp.float32, -1.0, 1.0)
    row_factor = jnp.exp(jax.random.uniform(keys[2], (count, width, BLK, 1), jnp.float32, -0.5, 0.47))
    col_factor = jnp.exp(jax.random.uniform(keys[3], (count, width, 1, BLK), jnp.float32, -0.5, 0.47))
    factor = (24.0 / ((LPB + RPB) * BLK)) ** 0.5
    return jnp.where(keep, entry * row_factor * col_factor * factor, 0.0).astype(jnp.bfloat16)


def draw_local_tiles(key, part):
    return tile_values(jax.random.fold_in(key, 11), NBLK, LPB)


def draw_remote_tiles(key, part):
    return tile_values(jax.random.fold_in(key, 23), NBLK, RPB)


def draw_remote_slots(key, part):
    keys = jax.random.split(jax.random.fold_in(key, 37), NBLK // NB)
    orders = jax.vmap(lambda k: jax.random.permutation(k, NB * RPB))(keys)
    return (orders % NRB).astype(jnp.int32).reshape(NBLK, RPB)


def draw_send_rows(key, part):
    devices = NBLK // NB
    stride = ROWS // SR
    jitter = jax.random.randint(jax.random.fold_in(key, 41), (devices, devices, SR), 0, stride)
    return (jitter + jnp.arange(SR, dtype=jnp.int32) * stride).astype(jnp.int32)


def touch_ends(drawn, key, smallest, largest):
    shape = drawn.shape
    index_at = [jax.random.randint(jax.random.fold_in(key, axis), (), 0, shape[axis]) for axis in range(len(shape))]
    drawn = drawn.at[tuple(index_at)].set(smallest)
    longest = shape.index(max(shape))
    index_at[longest] = (index_at[longest] + 1) % shape[longest]
    return drawn.at[tuple(index_at)].set(largest)


def steps_of(key, shape, pieces, least, largest):
    factor_of = 1.0
    for dim, parts in pieces:
        steps = jax.random.uniform(jax.random.fold_in(jax.random.fold_in(key, 6), dim), (parts,), jnp.float32, least / len(pieces), largest / len(pieces))
        factor_of = factor_of * jnp.repeat(jnp.exp(steps), shape[dim] // parts).reshape((-1,) + (1,) * (len(shape) - 1 - dim))
    return factor_of


def noise(key, extent, scale, limit, shards=(), kind=jnp.bfloat16):
    values = jax.random.normal(key, extent, jnp.float32) * scale
    if len(shards) > 0:
        values = steps_of(key, extent, shards, -0.22, 0.18) * values
    return jnp.clip(values, min=-limit, max=limit).astype(kind)


def setup_inputs(seed: int = 0) -> dict:
    arg_keys = jax.random.split(jax.random.key(seed), 13)
    features = noise(arg_keys[0], (NODES, FEAT), 1.0, 6.0, ((0, 128),))
    weight_in = noise(arg_keys[1], (FEAT, HID), FEAT ** -0.5, 0.5)
    bias_in = noise(arg_keys[2], (HID,), 0.5, 3.0, (), jnp.float32)
    weight_mid = noise(arg_keys[3], (HID, HID), HID ** -0.5, 0.375)
    bias_mid = noise(arg_keys[4], (HID,), 0.5, 3.0, (), jnp.float32)
    weight_out = noise(arg_keys[5], (HID, CLASSES), HID ** -0.5, 0.375)
    cotangent = noise(arg_keys[6], (NODES, CLASSES), 1.0, 6.0, ((0, 128),), jnp.float32)
    local_tiles = draw_local_tiles(jax.random.fold_in(arg_keys[12], 71), 0)
    local_columns = touch_ends(jax.random.randint(arg_keys[8], (NBLK, LPB), 0, NB), jax.random.fold_in(arg_keys[8], 1), 0, NB - 1).astype(jnp.int32)
    remote_tiles = draw_remote_tiles(jax.random.fold_in(arg_keys[12], 71), 0)
    remote_slots = draw_remote_slots(jax.random.fold_in(arg_keys[12], 71), 0)
    send_rows = draw_send_rows(jax.random.fold_in(arg_keys[12], 71), 0)
    return dict(features=features, weight_in=weight_in, bias_in=bias_in, weight_mid=weight_mid, bias_mid=bias_mid, weight_out=weight_out, cotangent=cotangent, local_tiles=local_tiles, local_columns=local_columns, remote_tiles=remote_tiles, remote_slots=remote_slots, send_rows=send_rows)


def silu_grad(value):
    sig = jax.nn.sigmoid(value)
    return sig * (1.0 + value * (1.0 - sig))

def reference(features, weight_in, bias_in, weight_mid, bias_mid, weight_out, cotangent, local_tiles, local_columns, remote_tiles, remote_slots, send_rows):
    devices = N_DP * N_SUB
    rows_dev = NB * BLK
    nodes = rows_dev * devices
    tiles_own = local_tiles.reshape(devices, NB, LPB, BLK, BLK)
    cols_own = local_columns.reshape(devices, NB, LPB)
    tiles_far = remote_tiles.reshape(devices, NB, RPB, BLK, BLK)
    slots_far = remote_slots.reshape(devices, NB, RPB)
    senders = jnp.arange(devices, dtype=jnp.int32)

    def propagate(values):
        blocks = values.reshape(devices, NB, BLK, CLASSES)

        def one_device(device):
            own = blocks[device]
            picked = own[cols_own[device]].astype(jnp.float32)
            summed = jnp.einsum('btij,btjc->bic', tiles_own[device].astype(jnp.float32), picked)
            rows = senders[:, None] * rows_dev + send_rows[:, device, :]
            received = values[rows].reshape(NRB, BLK, CLASSES)
            farpick = received[slots_far[device]].astype(jnp.float32)
            summed = summed + jnp.einsum('btij,btjc->bic', tiles_far[device].astype(jnp.float32), farpick)
            return 0.9 * summed
        result = lax.map(one_device, senders)
        return result.reshape(nodes, CLASSES)
    current = cotangent
    head_grad = 0.1 * cotangent
    for step in range(STEPS):
        current = propagate(current.astype(jnp.bfloat16))
        if step + 1 < STEPS:
            head_grad = head_grad + 0.1 * current
        else:
            head_grad = head_grad + current
    pre_in = jnp.dot(features, weight_in, preferred_element_type=jnp.float32) + bias_in
    hidden_in = jax.nn.silu(pre_in).astype(jnp.bfloat16)
    pre_mid = jnp.dot(hidden_in, weight_mid, preferred_element_type=jnp.float32) + bias_mid
    hidden_mid = jax.nn.silu(pre_mid).astype(jnp.bfloat16)
    delta_out = head_grad.astype(jnp.bfloat16)
    back_mid = jnp.dot(delta_out, weight_out.T, preferred_element_type=jnp.float32)
    delta_mid = (back_mid * silu_grad(pre_mid)).astype(jnp.bfloat16)
    back_in = jnp.dot(delta_mid, weight_mid.T, preferred_element_type=jnp.float32)
    delta_in = (back_in * silu_grad(pre_in)).astype(jnp.bfloat16)
    feature_grad = jnp.dot(delta_in, weight_in.T, preferred_element_type=jnp.float32)
    grad_scale = float(nodes) ** (-0.5)
    weight_out_grad = grad_scale * jnp.dot(hidden_mid.T, delta_out, preferred_element_type=jnp.float32)
    bias_out_grad = grad_scale * lax.optimization_barrier(jnp.sum(delta_out.astype(jnp.float32), axis=0))
    weight_mid_grad = grad_scale * jnp.dot(hidden_in.T, delta_mid, preferred_element_type=jnp.float32)
    bias_mid_grad = grad_scale * lax.optimization_barrier(jnp.sum(delta_mid.astype(jnp.float32), axis=0))
    weight_in_grad = grad_scale * jnp.dot(features.T, delta_in, preferred_element_type=jnp.float32)
    bias_in_grad = grad_scale * lax.optimization_barrier(jnp.sum(delta_in.astype(jnp.float32), axis=0))
    return (weight_in_grad, bias_in_grad, weight_mid_grad, bias_mid_grad, weight_out_grad, bias_out_grad, feature_grad)
```

```python
import jax
import jax.numpy as jnp
from jax import lax
from jax.experimental import pallas as pl
from jax.experimental.pallas import tpu as pltpu
from jax.sharding import PartitionSpec as P

STEPS = 3
MESH = pl.DeviceIdType.MESH
BF = jnp.bfloat16
F32 = jnp.float32
NDEV = 128
NB = 64
BLK = 128
ROWS = NB * BLK
CH = 256
FCH = 512
BCH = 1024
SLABS = (32, 32, 16, 1)
NSLAB = 81


def bdot(a, b):
    return jnp.dot(a, b, preferred_element_type=F32)


def kernel(
    feat, w_in, b_in, w_mid, b_mid, w_out, cot, ltile, lcol, rtile, rslot, srow,
    o_win, o_bin, o_wmid, o_bmid, o_wout, o_bout, o_fg,
    lt, rt, v, pf, stage, send, recv, vr, cring, fring,
    hmt, hit, xt, gi, gm,
    wi_s, bi_s, wm_s, bm_s, wo_s, wop, wot, wmt, wit,
    grad, rsr, gall,
    csem, fsem, tsem, wsem, ssem, rsem, gsem, grsem, asem, arsem, osem,
):
    dp = lax.axis_index("dp")
    sub = lax.axis_index("sub")
    z, x, core = dp // 8, (dp // 2) % 4, dp % 2
    me = dp * 4 + sub

    def target(i):
        dc, dy = i % 2, (i // 2) % 4
        dx = (i // 8 + i // 2) % 4
        dz = (i // 32 + i // 2 + i // 8) % 4
        return ((z + dz) % 4 * 4 + (x + dx) % 4) * 2 + (core + dc) % 2, (sub + dy) % 4

    def cot_copy(c):
        return pltpu.make_async_copy(cot.at[pl.ds(c * CH, CH)], cring.at[c % 4], csem.at[c % 4])

    def feat_copy(c):
        return pltpu.make_async_copy(feat.at[pl.ds(c * FCH, FCH)], fring.at[c % 2], fsem.at[c % 2])

    for c in range(4):
        cot_copy(c).start()
    small = [
        pltpu.make_async_copy(s, d, wsem.at[k])
        for k, (s, d) in enumerate(((w_in, wi_s), (b_in, bi_s), (w_mid, wm_s), (b_mid, bm_s), (w_out, wo_s)))
    ]
    for c in small:
        c.start()
    for c in range(2):
        feat_copy(c).start()

    barrier = pltpu.get_barrier_semaphore()

    def greet(i, _):
        a, b = target(i)
        pl.semaphore_signal(barrier, inc=1, device_id=(a, b), device_id_type=MESH)
        return 0

    lax.fori_loop(1, NDEV, greet, 0)
    tiles = (pltpu.make_async_copy(ltile, lt, tsem.at[0]), pltpu.make_async_copy(rtile, rt, tsem.at[1]))

    def load(c, _):
        cot_copy(c).wait()
        val = cring[c % 4]
        low = val[:, :128]
        high = jnp.concatenate([val[:, 128:172], jnp.zeros((CH, 84), F32)], axis=1)
        for k in range(CH // BLK):
            r = slice(k * BLK, (k + 1) * BLK)
            v[0, c * (CH // BLK) + k] = jnp.concatenate([low[r], high[r]], axis=1).astype(BF)
        base = pl.multiple_of(2 * CH * c, 2 * CH)
        pf[pl.ds(base, CH, stride=2), :] = low
        pf[pl.ds(base + 1, CH, stride=2), :] = high

        @pl.when(c + 4 < ROWS // CH)
        def _():
            cot_copy(c + 4).start()

        return 0

    lax.fori_loop(0, ROWS // CH, load, 0)
    for c in tiles:
        c.start()
    for c in small:
        c.wait()

    def pack(slot, t, g):
        for s in range(16):
            i = srow[0, t, s]
            stage[g, pl.ds(2 * s, 2), :] = pf[pl.ds(2 * i, 2), :]
        low = stage[g, pl.ds(0, 16, stride=2), :]
        hi0 = stage[g, pl.ds(1, 8, stride=2), :]
        hi1 = stage[g, pl.ds(17, 8, stride=2), :]
        hi = hi0 + pltpu.roll(hi1, 64, 1)
        send[slot, t] = jnp.concatenate([low, hi], axis=0).astype(BF)

    def dispatch(slot, t, a, b):
        pltpu.make_async_remote_copy(
            src_ref=send.at[slot, t], dst_ref=recv.at[slot, me], send_sem=ssem.at[slot], recv_sem=rsem.at[slot],
            device_id=(a, b), device_id_type=MESH,
        ).start()

    def own(slot):
        return pltpu.make_async_copy(send.at[slot, me], recv.at[slot, me], rsem.at[slot])

    wop[...] = jnp.zeros((256, 256), BF)
    wop[:, 0:172] = wo_s[...]
    wot[...] = wop[...].T
    wmt[...] = wm_s[...].T
    wit[...] = wi_s[...].T
    hmt[256:272, :] = jnp.ones((16, ROWS), BF)
    hit[256:272, :] = jnp.ones((16, ROWS), BF)
    xt[128:144, :] = jnp.ones((16, ROWS), BF)

    def act(pre):
        s = 0.5 * jnp.tanh(0.5 * pre) + 0.5
        h = pre * s
        return h.astype(BF), (s + h * (1.0 - s)).astype(BF)

    def forward(c, _):
        feat_copy(c).wait()
        f = fring[c % 2]
        cols = pl.ds(pl.multiple_of(c * FCH, FCH), FCH)
        xt[0:128, cols] = f.T
        h, g = act(bdot(f, wi_s[...]) + bi_s[...])
        gi[cols, :] = g
        hit[0:256, cols] = h.T
        h, g = act(bdot(h, wm_s[...]) + bm_s[...])
        gm[cols, :] = g
        hmt[0:256, cols] = h.T

        @pl.when(c + 2 < ROWS // FCH)
        def _():
            feat_copy(c + 2).start()

        return 0

    def local(k):
        def body(b, _):
            lhs = jnp.concatenate([lt[b, j] for j in range(4)], axis=1)
            rhs = jnp.concatenate([v[k, lcol[b, j]] for j in range(4)], axis=0)
            d = bdot(lhs, rhs)
            base = pl.multiple_of(2 * BLK * b, 2 * BLK)
            pf[pl.ds(base, BLK, stride=2), :] = d[:, :128]
            pf[pl.ds(base + 1, BLK, stride=2), :] = d[:, 128:]
            return 0

        lax.fori_loop(0, NB, body, 0)

    def unpack(slot):
        lane = lax.broadcasted_iota(jnp.int32, (8, 128), 1)

        def body(q, _):
            for u in range(8):
                m = recv[slot, q * 8 + u]
                hi = m[16:24].astype(F32)
                hi0 = jnp.where(lane < 64, hi, 0.0)
                hi1 = pltpu.roll(hi - hi0, 64, 1)
                vr[q, u * 16 : u * 16 + 16, 0:128] = m[0:16]
                vr[q, u * 16 : u * 16 + 16, 128:256] = jnp.concatenate([hi0, hi1], axis=0).astype(BF)
            return 0

        lax.fori_loop(0, 16, body, 0)

    def remote(k):
        def body(b, _):
            lhs = jnp.concatenate([rt[b, j] for j in range(2)], axis=1)
            rhs = jnp.concatenate([vr[rslot[b, j]] for j in range(2)], axis=0)
            d = bdot(lhs, rhs)
            base = pl.multiple_of(2 * BLK * b, 2 * BLK)
            low = 0.9 * (pf[pl.ds(base, BLK, stride=2), :] + d[:, :128])
            high = 0.9 * (pf[pl.ds(base + 1, BLK, stride=2), :] + d[:, 128:])
            p = jnp.concatenate([low, high], axis=1)
            if k + 1 < STEPS:
                pf[pl.ds(base, BLK, stride=2), :] = low
                pf[pl.ds(base + 1, BLK, stride=2), :] = high
                v[k + 1, b] = p.astype(BF)
            else:
                total = v[0, b].astype(F32) + v[1, b].astype(F32) + v[2, b].astype(F32)
                v[0, b] = (0.1 * total + p).astype(BF)
            return 0

        lax.fori_loop(0, NB, body, 0)

    def whole_send(slot):
        return pltpu.make_async_copy(
            send.at[slot, pl.ds(0, NDEV - 1)], recv.at[slot, pl.ds(0, NDEV - 1)], ssem.at[slot])

    def whole_recv(slot):
        return pltpu.make_async_copy(send.at[slot], recv.at[slot], rsem.at[slot])

    def pack_all(i, _):
        pack(0, i, i % 4)
        return 0

    lax.fori_loop(0, NDEV, pack_all, 0)
    lax.fori_loop(0, 8, forward, 0)
    pl.semaphore_wait(barrier, NDEV - 1)
    own(0).start()

    def send_all(i, _):
        a, b = target(i)
        dispatch(0, a * 4 + b, a, b)
        return 0

    lax.fori_loop(1, NDEV, send_all, 0)
    for c in tiles:
        c.wait()
    for k in range(STEPS):
        slot = k % 2
        if k > 0:
            if k >= 2:
                whole_send(slot).wait()
            pack(slot, me, 0)
            own(slot).start()

            def pack_send(i, _, slot=slot):
                a, b = target(i)
                pack(slot, a * 4 + b, i % 4)
                dispatch(slot, a * 4 + b, a, b)
                return 0

            lax.fori_loop(1, NDEV, pack_send, 0)
        local(k)
        if k == 0:
            lax.fori_loop(8, 12, forward, 0)
        elif k == 1:
            lax.fori_loop(12, 16, forward, 0)
        whole_recv(slot).wait()
        unpack(slot)
        remote(k)
    for slot in (1, 0):
        whole_send(slot).wait()

    nb = BCH // BLK
    scale = float(ROWS * NDEV) ** -0.5
    grad[...] = jnp.zeros_like(grad)

    def delta(c):
        return jnp.concatenate([v[0, c * nb + j] for j in range(nb)], axis=0)

    def add(first, count, bias, d):
        for s in range(count):
            grad[first + s] += d[8 * s : 8 * s + 8]
        grad[NSLAB - 1, pl.ds(bias, 1), :] += d[8 * count : 8 * count + 1]

    def out_grad(c, _):
        cols = pl.ds(pl.multiple_of(c * BCH, BCH), BCH)
        add(0, 32, 0, bdot(hmt[:, cols], delta(c)))
        return 0

    def mid_grad(c, _):
        cols = pl.ds(pl.multiple_of(c * BCH, BCH), BCH)
        dm = (bdot(delta(c), wot[...]) * gm[cols, :].astype(F32)).astype(BF)
        gm[cols, :] = dm
        add(32, 32, 1, bdot(hit[:, cols], dm))
        return 0

    def in_grad(c, _):
        cols = pl.ds(pl.multiple_of(c * BCH, BCH), BCH)
        di = (bdot(gm[cols, :], wmt[...]) * gi[cols, :].astype(F32)).astype(BF)
        gi[cols, :] = di
        add(64, 16, 2, bdot(xt[:, cols], di))
        return 0

    def owner(s):
        return (s * 3) % NDEV

    def scatter(first, count, sem):
        def body(s, _):
            o = owner(s)

            @pl.when(o != me)
            def _():
                pltpu.make_async_remote_copy(
                    src_ref=grad.at[s], dst_ref=rsr.at[me], send_sem=gsem.at[0], recv_sem=grsem.at[0],
                    device_id=(o // 4, o % 4), device_id_type=MESH,
                ).start()

            @pl.when(o == me)
            def _():
                pltpu.make_async_copy(grad.at[s], rsr.at[me], grsem.at[0]).start()

            return 0

        lax.fori_loop(first, first + count, body, 0)

    lax.fori_loop(0, ROWS // BCH, out_grad, 0)
    scatter(0, 32, 0)
    lax.fori_loop(0, ROWS // BCH, mid_grad, 0)
    scatter(32, 32, 0)
    lax.fori_loop(0, ROWS // BCH, in_grad, 0)
    scatter(64, 17, 0)

    def feature(c, _):
        cols = pl.ds(pl.multiple_of(c * BCH, BCH), BCH)
        pf[cols, :] = bdot(gi[cols, :], wit[...])
        pltpu.make_async_copy(pf.at[cols], o_fg.at[cols], osem).start()
        return 0

    lax.fori_loop(0, ROWS // BCH, feature, 0)

    inverse = (me * 43) % NDEV
    mine = inverse < NSLAB

    @pl.when(mine)
    def _():
        pltpu.make_async_copy(rsr, rsr, grsem.at[0]).wait()

        def body(i, acc):
            part = [rsr[i * 8 + j] for j in range(8)]
            while len(part) > 1:
                part = [part[j] + part[j + 1] for j in range(0, len(part), 2)]
            return acc + part[0]

        total = lax.fori_loop(0, NDEV // 8, body, jnp.zeros((8, 256), F32))
        gall[inverse] = scale * total

        def spread(i, _):
            a, b = target(i)
            pltpu.make_async_remote_copy(
                src_ref=gall.at[inverse], dst_ref=gall.at[inverse], send_sem=asem.at[0], recv_sem=arsem.at[0],
                device_id=(a, b), device_id_type=MESH,
            ).start()
            return 0

        lax.fori_loop(1, NDEV, spread, 0)
        pltpu.make_async_copy(gall.at[pl.ds(0, NSLAB - 1)], gall.at[pl.ds(0, NSLAB - 1)], arsem.at[0]).wait()
        pltpu.make_async_copy(rsr.at[pl.ds(0, NDEV - 1)], rsr.at[pl.ds(0, NDEV - 1)], asem.at[0]).wait()
        pltpu.make_async_copy(gall.at[pl.ds(0, NSLAB - 1)], gall.at[pl.ds(0, NSLAB - 1)], gsem.at[0]).wait()

    @pl.when(jnp.logical_not(mine))
    def _():
        pltpu.make_async_copy(gall, gall, arsem.at[0]).wait()
        pltpu.make_async_copy(gall, gall, gsem.at[0]).wait()

    for s in range(32):
        o_wout[8 * s : 8 * s + 8, :] = gall[s][:, 0:172]
        o_wmid[8 * s : 8 * s + 8, :] = gall[32 + s]
    for s in range(16):
        o_win[8 * s : 8 * s + 8, :] = gall[64 + s]
    o_bout[...] = gall[NSLAB - 1, 0:1, 0:172]
    o_bmid[...] = gall[NSLAB - 1, 1:2, :]
    o_bin[...] = gall[NSLAB - 1, 2:3, :]
    pltpu.make_async_copy(pf.at[pl.ds(0, ROWS)], o_fg, osem).wait()


def shards(
    features, weight_in, bias_in, weight_mid, bias_mid, weight_out, cotangent,
    local_tiles, local_columns, remote_tiles, remote_slots, send_rows,
):
    any_ = pl.BlockSpec(memory_space=pl.ANY)
    smem = pl.BlockSpec(memory_space=pltpu.SMEM)
    vmem = pl.BlockSpec(memory_space=pltpu.VMEM)
    dma = pltpu.SemaphoreType.DMA
    win, bi, wmid, bm, wout, bo, fg = pl.pallas_call(
        kernel,
        out_shape=[
            jax.ShapeDtypeStruct(s, F32)
            for s in ((128, 256), (1, 256), (256, 256), (1, 256), (256, 172), (1, 172), (ROWS, 128))
        ],
        in_specs=[any_] * 8 + [smem, any_, smem, smem],
        out_specs=[vmem] * 6 + [any_],
        scratch_shapes=[
            pltpu.VMEM((NB, 4, BLK, BLK), BF),
            pltpu.VMEM((NB, 2, BLK, BLK), BF),
            pltpu.VMEM((3, NB, BLK, 256), BF),
            pltpu.VMEM((2 * ROWS, 128), F32),
            pltpu.VMEM((4, 32, 128), F32),
            pltpu.VMEM((2, NDEV, 24, 128), BF),
            pltpu.VMEM((2, NDEV, 24, 128), BF),
            pltpu.VMEM((16, BLK, 256), BF),
            pltpu.VMEM((4, CH, 172), F32),
            pltpu.VMEM((2, FCH, 128), BF),
            pltpu.VMEM((272, ROWS), BF),
            pltpu.VMEM((272, ROWS), BF),
            pltpu.VMEM((144, ROWS), BF),
            pltpu.VMEM((ROWS, 256), BF),
            pltpu.VMEM((ROWS, 256), BF),
            pltpu.VMEM((128, 256), BF),
            pltpu.VMEM((1, 256), F32),
            pltpu.VMEM((256, 256), BF),
            pltpu.VMEM((1, 256), F32),
            pltpu.VMEM((256, 172), BF),
            pltpu.VMEM((256, 256), BF),
            pltpu.VMEM((256, 256), BF),
            pltpu.VMEM((256, 256), BF),
            pltpu.VMEM((256, 128), BF),
            pltpu.VMEM((NSLAB, 8, 256), F32),
            pltpu.VMEM((NDEV, 8, 256), F32),
            pltpu.VMEM((NSLAB, 8, 256), F32),
            dma((4,)), dma((2,)), dma((2,)), dma((5,)), dma((2,)), dma((2,)),
            dma((1,)), dma((1,)), dma((1,)), dma((1,)), dma,
        ],
        compiler_params=pltpu.CompilerParams(
            collective_id=0, has_side_effects=True, vmem_limit_bytes=63 * 2**20
        ),
        cost_estimate=pl.CostEstimate(flops=13 * 10**9, bytes_accessed=30 * 10**6, transcendentals=4 * 10**6),
        name="appnp_backward",
    )(
        features, weight_in, bias_in.reshape(1, 256), weight_mid, bias_mid.reshape(1, 256), weight_out, cotangent,
        local_tiles, local_columns, remote_tiles, remote_slots, send_rows,
    )
    return win, bi.reshape(256), wmid, bm.reshape(256), wout, bo.reshape(172), fg


def solution(mesh):
    both = ("dp", "sub")
    return jax.shard_map(
        shards,
        mesh=mesh,
        in_specs=(
            P(both, None), P(), P(), P(), P(), P(), P(both, None), P(both, None, None, None),
            P(both, None), P(both, None, None, None), P(both, None), P(both, None, None),
        ),
        out_specs=(P(), P(), P(), P(), P(), P(), P(both, None)),
        check_vma=False,
    )
```

```python
import jax
import jax.numpy as jnp
from jax import lax
from jax.experimental import pallas as pl
from jax.experimental.pallas import tpu as pltpu
from jax.sharding import PartitionSpec as P

STEPS = 3
MESH = pl.DeviceIdType.MESH
BF = jnp.bfloat16
F32 = jnp.float32
NDEV = 128
NB = 64
BLK = 128
ROWS = NB * BLK
CH = 512
FCH = 512
BCH = 1024
SLABS = (32, 32, 16, 1)
NSLAB = 81
UL = 4
UR = 8
UP = 4


def bdot(a, b):
    return jnp.dot(a, b, preferred_element_type=F32)


def kernel(
    feat, w_in, b_in, w_mid, b_mid, w_out, cot, ltile, lcol, rtile, rslot, srow,
    o_grad, o_di,
    lt, rt, v, pf, stage, send, recv, vr, cring, fring,
    hmt, hit, xt, gi, gm,
    wi_s, bi_s, wm_s, bm_s, wo_s, wot, wmt,
    grad, rsr, gall,
    csem, fsem, tsem, wsem, ssem, rsem, gsem, grsem, asem, arsem, osem,
):
    dp = lax.axis_index("dp")
    sub = lax.axis_index("sub")
    me = dp * 4 + sub

    def target(i):
        t = lax.rem(me + i, NDEV)
        return t, lax.div(t, 4), lax.rem(t, 4)

    def cot_copy(c):
        return pltpu.make_async_copy(cot.at[:, pl.ds(pl.multiple_of(c * CH, CH), CH)], cring.at[c % 4], csem.at[c % 4])

    def feat_copy(c):
        return pltpu.make_async_copy(feat.at[pl.ds(c * FCH, FCH)], fring.at[c % 2], fsem.at[c % 2])

    for c in range(4):
        cot_copy(c).start()
    small = [
        pltpu.make_async_copy(s, d, wsem.at[k])
        for k, (s, d) in enumerate(((w_in, wi_s), (b_in, bi_s), (w_mid, wm_s), (b_mid, bm_s), (w_out, wo_s)))
    ]
    for c in small:
        c.start()
    for c in range(2):
        feat_copy(c).start()

    barrier = pltpu.get_barrier_semaphore()

    def greet(i, _):
        _, a, b = target(i)
        pl.semaphore_signal(barrier, inc=1, device_id=(a, b), device_id_type=MESH)
        return 0

    lax.fori_loop(1, NDEV, greet, 0)
    tiles = (pltpu.make_async_copy(ltile, lt, tsem.at[0]), pltpu.make_async_copy(rtile, rt, tsem.at[1]))

    row = lax.broadcasted_iota(jnp.int32, (256, 256), 0)
    eye = (row == lax.broadcasted_iota(jnp.int32, (256, 256), 1)).astype(F32).astype(BF)

    def load_compute(c):
        val = jnp.concatenate([cring[c % 4], jnp.zeros((84, CH), F32)], axis=0).astype(BF)
        for h in range(CH // 256):
            part = val[:, 256 * h : 256 * h + 256]
            d = lax.dot_general(eye, part, (((1,), (1,)), ((), ())), preferred_element_type=F32)
            for k in range(2):
                v[0, c * (CH // BLK) + 2 * h + k] = d[BLK * k : BLK * k + BLK].astype(BF)
            base = pl.multiple_of(2 * CH * c + 512 * h, 512)
            pf[pl.ds(base, 256, stride=2), :] = d[:, :128]
            pf[pl.ds(base + 1, 256, stride=2), :] = d[:, 128:]

    def load(c, _):
        cot_copy(c).wait()
        load_compute(c)

        @pl.when(c + 4 < ROWS // CH)
        def _():
            cot_copy(c + 4).start()

        return 0

    lax.fori_loop(0, ROWS // CH, load, 0)
    for c in tiles:
        c.start()
    for c in small:
        c.wait()

    def pack(slot, t, g):
        for s in range(16):
            i = srow[0, s, t]
            stage[g, pl.ds(2 * s, 2), :] = pf[pl.ds(2 * i, 2), :]
        low = stage[g, pl.ds(0, 16, stride=2), :]
        hi0 = stage[g, pl.ds(1, 8, stride=2), :]
        hi1 = stage[g, pl.ds(17, 8, stride=2), :]
        hi = hi0 + pltpu.roll(hi1, 64, 1)
        send[slot, t] = jnp.concatenate([low, hi], axis=0).astype(BF)

    def dispatch(slot, t, a, b):
        pltpu.make_async_remote_copy(
            src_ref=send.at[slot, t], dst_ref=recv.at[slot, me], send_sem=ssem.at[slot], recv_sem=rsem.at[slot],
            device_id=(a, b), device_id_type=MESH,
        ).start()

    def own(slot):
        return pltpu.make_async_copy(send.at[slot, me], recv.at[slot, me], rsem.at[slot])

    wot[...] = jnp.zeros((256, 256), BF)
    wot[0:172, :] = wo_s[...]
    wmt[...] = wm_s[...].T
    hmt[256:272, :] = jnp.ones((16, ROWS), BF)
    hit[256:272, :] = jnp.ones((16, ROWS), BF)
    xt[128:144, :] = jnp.ones((16, ROWS), BF)

    def act(pre):
        s = 0.5 * jnp.tanh(0.5 * pre) + 0.5
        h = pre * s
        return h.astype(BF), (s + h * (1.0 - s)).astype(BF)

    def forward(c, _):
        feat_copy(c).wait()
        f = fring[c % 2]
        cols = pl.ds(pl.multiple_of(c * FCH, FCH), FCH)
        xt[0:128, cols] = f.T
        h, g = act(bdot(f, wi_s[...]) + bi_s[...])
        gi[cols, :] = g
        hit[0:256, cols] = h.T
        h, g = act(bdot(h, wm_s[...]) + bm_s[...])
        gm[cols, :] = g
        hmt[0:256, cols] = h.T

        @pl.when(c + 2 < ROWS // FCH)
        def _():
            feat_copy(c + 2).start()

        return 0

    def local(k):
        def body(i, _):
            for u in range(UL):
                b = i * UL + u
                lhs = jnp.concatenate([lt[b, j] for j in range(4)], axis=1)
                rhs = jnp.concatenate([v[k, lcol[j, b]] for j in range(4)], axis=0)
                d = bdot(lhs, rhs)
                base = pl.multiple_of(2 * BLK * b, 2 * BLK)
                pf[pl.ds(base, BLK, stride=2), :] = d[:, :128]
                pf[pl.ds(base + 1, BLK, stride=2), :] = d[:, 128:]
            return 0

        lax.fori_loop(0, NB // UL, body, 0)

    def unpack(slot):
        lane = lax.broadcasted_iota(jnp.int32, (8, 128), 1)

        def body(q, _):
            for u in range(8):
                m = recv[slot, q * 8 + u]
                hi = m[16:24].astype(F32)
                hi0 = jnp.where(lane < 64, hi, 0.0)
                hi1 = pltpu.roll(hi - hi0, 64, 1)
                vr[q, u * 16 : u * 16 + 16, 0:128] = m[0:16]
                vr[q, u * 16 : u * 16 + 16, 128:256] = jnp.concatenate([hi0, hi1], axis=0).astype(BF)
            return 0

        lax.fori_loop(0, 16, body, 0)

    def remote(k):
        def body(i, _):
            ds = []
            for u in range(UR):
                b = i * UR + u
                lhs = jnp.concatenate([rt[b, j] for j in range(2)], axis=1)
                rhs = jnp.concatenate([vr[rslot[j, b]] for j in range(2)], axis=0)
                ds.append(bdot(lhs, rhs))
            for u in range(UR):
                b, d = i * UR + u, ds[u]
                base = pl.multiple_of(2 * BLK * b, 2 * BLK)
                low = 0.9 * (pf[pl.ds(base, BLK, stride=2), :] + d[:, :128])
                high = 0.9 * (pf[pl.ds(base + 1, BLK, stride=2), :] + d[:, 128:])
                p = jnp.concatenate([low, high], axis=1)
                if k + 1 < STEPS:
                    pf[pl.ds(base, BLK, stride=2), :] = low
                    pf[pl.ds(base + 1, BLK, stride=2), :] = high
                    v[k + 1, b] = p.astype(BF)
                else:
                    total = v[0, b].astype(F32) + v[1, b].astype(F32) + v[2, b].astype(F32)
                    v[0, b] = (0.1 * total + p).astype(BF)
            return 0

        lax.fori_loop(0, NB // UR, body, 0)

    def whole_send(slot):
        return pltpu.make_async_copy(
            send.at[slot, pl.ds(0, NDEV - 1)], recv.at[slot, pl.ds(0, NDEV - 1)], ssem.at[slot])

    def whole_recv(slot):
        return pltpu.make_async_copy(send.at[slot], recv.at[slot], rsem.at[slot])

    def pack_all(i, _):
        for u in range(UP):
            pack(0, i * UP + u, u)
        return 0

    lax.fori_loop(0, NDEV // UP, pack_all, 0)
    lax.fori_loop(0, 8, forward, 0)
    pl.semaphore_wait(barrier, NDEV - 1)
    own(0).start()

    def send_all(i, _):
        t, a, b = target(i)
        dispatch(0, t, a, b)
        return 0

    lax.fori_loop(1, NDEV, send_all, 0)
    for c in tiles:
        c.wait()
    for k in range(STEPS):
        slot = k % 2
        if k > 0:
            if k >= 2:
                whole_send(slot).wait()

            def pack_send(i, first, slot=slot):
                at = [target(i * UP + u) for u in range(first, UP)]
                for u, (t, a, b) in enumerate(at):
                    pack(slot, t, u + first)
                for t, a, b in at:
                    dispatch(slot, t, a, b)
                return 0

            pack_send(0, 1)
            pack(slot, me, 0)
            own(slot).start()
            lax.fori_loop(1, NDEV // UP, lambda i, _: pack_send(i, 0), 0)
        local(k)
        if k == 0:
            lax.fori_loop(8, 12, forward, 0)
        elif k == 1:
            lax.fori_loop(12, 16, forward, 0)
        whole_recv(slot).wait()
        unpack(slot)
        remote(k)
    for slot in (1, 0):
        whole_send(slot).wait()

    nb = BCH // BLK
    scale = float(ROWS * NDEV) ** -0.5
    grad[...] = jnp.zeros_like(grad)

    def delta(c):
        return jnp.concatenate([v[0, c * nb + j] for j in range(nb)], axis=0)

    def add(first, count, bias, d):
        for s in range(count):
            grad[first + s] += d[8 * s : 8 * s + 8]
        grad[NSLAB - 1, pl.ds(bias, 1), :] += d[8 * count : 8 * count + 1]

    def out_grad(c, _):
        cols = pl.ds(pl.multiple_of(c * BCH, BCH), BCH)
        add(0, 32, 0, bdot(hmt[:, cols], delta(c)))
        return 0

    def mid_grad(c, _):
        cols = pl.ds(pl.multiple_of(c * BCH, BCH), BCH)
        dm = (bdot(delta(c), wot[...]) * gm[cols, :].astype(F32)).astype(BF)
        gm[cols, :] = dm
        add(32, 32, 1, bdot(hit[:, cols], dm))
        return 0

    def in_grad(c, _):
        cols = pl.ds(pl.multiple_of(c * BCH, BCH), BCH)
        di = (bdot(gm[cols, :], wmt[...]) * gi[cols, :].astype(F32)).astype(BF)
        gi[cols, :] = di
        add(64, 16, 2, bdot(xt[:, cols], di))
        return 0

    def owner(s):
        return (s * 3) % NDEV

    def scatter(first, count, sem):
        def body(i, _):
            s = first + i
            o = owner(s)

            @pl.when(o != me)
            def _():
                pltpu.make_async_remote_copy(
                    src_ref=grad.at[s], dst_ref=rsr.at[me], send_sem=gsem.at[0], recv_sem=grsem.at[0],
                    device_id=(o // 4, o % 4), device_id_type=MESH,
                ).start()

            @pl.when(o == me)
            def _():
                pltpu.make_async_copy(grad.at[s], rsr.at[me], grsem.at[0]).start()

            return 0

        lax.fori_loop(0, count, body, 0)

    lax.fori_loop(0, ROWS // BCH, out_grad, 0)
    scatter(0, 32, 0)
    lax.fori_loop(0, ROWS // BCH, mid_grad, 0)
    scatter(32, 32, 0)
    lax.fori_loop(0, ROWS // BCH, in_grad, 0)
    scatter(64, 17, 0)

    out_di = pltpu.make_async_copy(gi, o_di, osem)
    out_di.start()

    inverse = (me * 43) % NDEV
    mine = inverse < NSLAB

    @pl.when(mine)
    def _():
        pltpu.make_async_copy(rsr, rsr, grsem.at[0]).wait()

        def body(i, acc):
            part = [rsr[i * 8 + j] for j in range(8)]
            while len(part) > 1:
                part = [part[j] + part[j + 1] for j in range(0, len(part), 2)]
            return acc + part[0]

        total = lax.fori_loop(0, NDEV // 8, body, jnp.zeros((8, 256), F32))
        total = scale * total
        gall[inverse] = jnp.concatenate([total[:, :128], total[:, 128:]], axis=0).astype(BF)

        def spread(i, _):
            _, a, b = target(i)
            pltpu.make_async_remote_copy(
                src_ref=gall.at[inverse], dst_ref=gall.at[inverse], send_sem=asem.at[0], recv_sem=arsem.at[0],
                device_id=(a, b), device_id_type=MESH,
            ).start()
            return 0

        lax.fori_loop(1, NDEV, spread, 0)
        pltpu.make_async_copy(gall.at[pl.ds(0, NSLAB - 1)], gall.at[pl.ds(0, NSLAB - 1)], arsem.at[0]).wait()
        pltpu.make_async_copy(recv.at[0, pl.ds(0, NDEV - 1), pl.ds(0, 16)], recv.at[0, pl.ds(0, NDEV - 1), pl.ds(0, 16)], asem.at[0]).wait()
        pltpu.make_async_copy(grad.at[pl.ds(0, NSLAB - 1)], grad.at[pl.ds(0, NSLAB - 1)], gsem.at[0]).wait()

    @pl.when(jnp.logical_not(mine))
    def _():
        pltpu.make_async_copy(gall, gall, arsem.at[0]).wait()
        pltpu.make_async_copy(grad, grad, gsem.at[0]).wait()

    o_grad[...] = gall[...]
    out_di.wait()


def finish(grad, di, w_in, o_win, o_bin, o_wmid, o_bmid, o_wout, o_bout, o_fg):
    o_fg[...] = lax.dot_general(di[...], w_in[...], (((1,), (1,)), ((), ())), preferred_element_type=F32)

    def slabs(first, count):
        parts = [grad[s].astype(F32) for s in range(first, first + count)]
        low = jnp.concatenate([p[0:8] for p in parts], axis=0)
        high = jnp.concatenate([p[8:16] for p in parts], axis=0)
        return jnp.concatenate([low, high], axis=1)

    @pl.when(pl.program_id(0) == 0)
    def _():
        o_wout[...] = slabs(0, 32).T[0:172]
        o_wmid[...] = slabs(32, 32)
        o_win[...] = slabs(64, 16)
        bias = slabs(NSLAB - 1, 1)
        o_bout[...] = bias[0:1, 0:172]
        o_bmid[...] = bias[1:2]
        o_bin[...] = bias[2:3]


def shards(
    features, weight_in, bias_in, weight_mid, bias_mid, weight_out, cotangent,
    local_tiles, local_columns, remote_tiles, remote_slots, send_rows,
):
    any_ = pl.BlockSpec(memory_space=pl.ANY)
    smem = pl.BlockSpec(memory_space=pltpu.SMEM)
    vmem = pl.BlockSpec(memory_space=pltpu.VMEM)
    dma = pltpu.SemaphoreType.DMA
    grad, di = pl.pallas_call(
        kernel,
        out_shape=[jax.ShapeDtypeStruct((NSLAB, 16, 128), BF), jax.ShapeDtypeStruct((ROWS, 256), BF)],
        in_specs=[any_] * 8 + [smem, any_, smem, smem],
        out_specs=[vmem, any_],
        scratch_shapes=[
            pltpu.VMEM((NB, 4, BLK, BLK), BF),
            pltpu.VMEM((NB, 2, BLK, BLK), BF),
            pltpu.VMEM((3, NB, BLK, 256), BF),
            pltpu.VMEM((2 * ROWS, 128), F32),
            pltpu.VMEM((UP, 32, 128), F32),
            pltpu.VMEM((2, NDEV, 24, 128), BF),
            pltpu.VMEM((2, NDEV, 24, 128), BF),
            pltpu.VMEM((16, BLK, 256), BF),
            pltpu.VMEM((4, 172, CH), F32),
            pltpu.VMEM((2, FCH, 128), BF),
            pltpu.VMEM((272, ROWS), BF),
            pltpu.VMEM((272, ROWS), BF),
            pltpu.VMEM((144, ROWS), BF),
            pltpu.VMEM((ROWS, 256), BF),
            pltpu.VMEM((ROWS, 256), BF),
            pltpu.VMEM((128, 256), BF),
            pltpu.VMEM((1, 256), F32),
            pltpu.VMEM((256, 256), BF),
            pltpu.VMEM((1, 256), F32),
            pltpu.VMEM((172, 256), BF),
            pltpu.VMEM((256, 256), BF),
            pltpu.VMEM((256, 256), BF),
            pltpu.VMEM((NSLAB, 8, 256), F32),
            pltpu.VMEM((NDEV, 8, 256), F32),
            pltpu.VMEM((NSLAB, 16, 128), BF),
            dma((4,)), dma((2,)), dma((2,)), dma((5,)), dma((2,)), dma((2,)),
            dma((1,)), dma((1,)), dma((1,)), dma((1,)), dma,
        ],
        compiler_params=pltpu.CompilerParams(
            collective_id=0, has_side_effects=True, vmem_limit_bytes=63 * 2**20
        ),
        cost_estimate=pl.CostEstimate(flops=13 * 10**9, bytes_accessed=30 * 10**6, transcendentals=4 * 10**6),
        name="appnp_backward",
    )(
        features, weight_in, bias_in.reshape(1, 256), weight_mid, bias_mid.reshape(1, 256), weight_out.T, cotangent.T,
        local_tiles, local_columns.T, remote_tiles, remote_slots.T, send_rows.transpose(0, 2, 1),
    )
    fch = 1024
    win, bi, wmid, bm, wout, bo, fg = pl.pallas_call(
        finish,
        grid=(ROWS // fch,),
        out_shape=[
            jax.ShapeDtypeStruct(s, F32)
            for s in ((128, 256), (1, 256), (256, 256), (1, 256), (172, 256), (1, 172), (ROWS, 128))
        ],
        in_specs=[vmem, pl.BlockSpec((fch, 256), lambda i: (i, 0)), vmem],
        out_specs=[vmem] * 6 + [pl.BlockSpec((fch, 128), lambda i: (i, 0))],
        name="finish",
    )(grad, di, weight_in)
    return win, bi.reshape(256), wmid, bm.reshape(256), wout.T, bo.reshape(172), fg


def solution(mesh):
    both = ("dp", "sub")
    return jax.shard_map(
        shards,
        mesh=mesh,
        in_specs=(
            P(both, None), P(), P(), P(), P(), P(), P(both, None), P(both, None, None, None),
            P(both, None), P(both, None, None, None), P(both, None), P(both, None, None),
        ),
        out_specs=(P(), P(), P(), P(), P(), P(), P(both, None)),
        check_vma=False,
    )
```

```python
import jax
import jax.numpy as jnp
from jax import lax
from jax.experimental import pallas as pl
from jax.experimental.pallas import tpu as pltpu
from jax.sharding import PartitionSpec as P

STEPS = 3
MESH = pl.DeviceIdType.MESH
BF = jnp.bfloat16
F32 = jnp.float32
NDEV = 128
NB = 64
BLK = 128
ROWS = NB * BLK
CH = 512
FCH = 512
BCH = 4096
SLABS = (32, 32, 16, 1)
NSLAB = 81
F1 = 5
F2 = 10
UL = 4
UR = 8
UP = 4


def bdot(a, b):
    return jnp.dot(a, b, preferred_element_type=F32)


def kernel(
    feat, w_in, b_in, w_mid, b_mid, w_out, cot, ltile, lcol, rtile, rslot, srow,
    o_grad, o_di,
    lt, rt, v, pf, stage, send, recv, vr, cring, fring,
    hmt, hit, xt, gi, gm,
    wi_s, bi_s, wm_s, bm_s, wo_s, wot, wmt,
    grad, rsr, gall,
    csem, fsem, tsem, wsem, ssem, rsem, gsem, grsem, asem, arsem, osem,
):
    dp = lax.axis_index("dp")
    sub = lax.axis_index("sub")
    me = dp * 4 + sub
    block = lax.div(me, 8)

    def target(i):
        t = lax.rem(me + i, NDEV)
        return t, lax.div(t, 4), lax.rem(t, 4)

    def cot_copy(c):
        return pltpu.make_async_copy(cot.at[:, pl.ds(pl.multiple_of(c * CH, CH), CH)], cring.at[c % 4], csem.at[c % 4])

    def feat_copy(c):
        return pltpu.make_async_copy(feat.at[pl.ds(c * FCH, FCH)], fring.at[c % 2], fsem.at[c % 2])

    for c in range(4):
        cot_copy(c).start()
    small = [
        pltpu.make_async_copy(s, d, wsem.at[k])
        for k, (s, d) in enumerate(((w_in, wi_s), (b_in, bi_s), (w_mid, wm_s), (b_mid, bm_s), (w_out, wo_s)))
    ]
    for c in small:
        c.start()
    for c in range(2):
        feat_copy(c).start()

    barrier = pltpu.get_barrier_semaphore()

    def greet(i, _):
        _, a, b = target(i)
        pl.semaphore_signal(barrier, inc=1, device_id=(a, b), device_id_type=MESH)
        return 0

    lax.fori_loop(1, NDEV, greet, 0)
    tiles = (pltpu.make_async_copy(ltile, lt, tsem.at[0]), pltpu.make_async_copy(rtile, rt, tsem.at[1]))

    row = lax.broadcasted_iota(jnp.int32, (256, 256), 0)
    eye = (row == lax.broadcasted_iota(jnp.int32, (256, 256), 1)).astype(F32).astype(BF)

    def load_compute(c):
        val = jnp.concatenate([cring[c % 4], jnp.zeros((84, CH), F32)], axis=0).astype(BF)
        for h in range(CH // 256):
            part = val[:, 256 * h : 256 * h + 256]
            d = lax.dot_general(eye, part, (((1,), (1,)), ((), ())), preferred_element_type=F32)
            for k in range(2):
                v[0, c * (CH // BLK) + 2 * h + k] = d[BLK * k : BLK * k + BLK].astype(BF)
            base = pl.multiple_of(2 * CH * c + 512 * h, 512)
            pf[pl.ds(base, 256, stride=2), :] = d[:, :128]
            pf[pl.ds(base + 1, 256, stride=2), :] = d[:, 128:]

    def load(c, _):
        cot_copy(c).wait()
        load_compute(c)

        @pl.when(c + 4 < ROWS // CH)
        def _():
            cot_copy(c + 4).start()

        return 0

    lax.fori_loop(0, ROWS // CH, load, 0)
    for c in tiles:
        c.start()
    for c in small:
        c.wait()

    def pack(slot, t, g):
        for s in range(16):
            i = srow[0, s, t]
            stage[g, pl.ds(2 * s, 2), :] = pf[pl.ds(2 * i, 2), :]
        low = stage[g, pl.ds(0, 16, stride=2), :]
        hi0 = stage[g, pl.ds(1, 8, stride=2), :]
        hi1 = stage[g, pl.ds(17, 8, stride=2), :]
        hi = hi0 + pltpu.roll(hi1, 64, 1)
        send[slot, t] = jnp.concatenate([low, hi], axis=0).astype(BF)

    def dispatch(slot, t, a, b):
        pltpu.make_async_remote_copy(
            src_ref=send.at[slot, t], dst_ref=recv.at[slot, me], send_sem=ssem.at[slot], recv_sem=rsem.at[slot, block],
            device_id=(a, b), device_id_type=MESH,
        ).start()

    def own(slot):
        return pltpu.make_async_copy(send.at[slot, me], recv.at[slot, me], rsem.at[slot, block])

    wot[...] = jnp.zeros((256, 256), BF)
    wot[0:172, :] = wo_s[...]
    wmt[...] = wm_s[...].T
    hmt[256:272, :] = jnp.ones((16, ROWS), BF)
    hit[256:272, :] = jnp.ones((16, ROWS), BF)
    xt[128:144, :] = jnp.ones((16, ROWS), BF)

    def act(pre):
        s = 0.5 * jnp.tanh(0.5 * pre) + 0.5
        h = pre * s
        return h.astype(BF), (s + h * (1.0 - s)).astype(BF)

    def forward(c, _):
        feat_copy(c).wait()
        f = fring[c % 2]
        cols = pl.ds(pl.multiple_of(c * FCH, FCH), FCH)
        xt[0:128, cols] = f.T
        h, g = act(bdot(f, wi_s[...]) + bi_s[...])
        gi[cols, :] = g
        hit[0:256, cols] = h.T
        h, g = act(bdot(h, wm_s[...]) + bm_s[...])
        gm[cols, :] = g
        hmt[0:256, cols] = h.T

        @pl.when(c + 2 < ROWS // FCH)
        def _():
            feat_copy(c + 2).start()

        return 0

    def local(k):
        def body(i, _):
            for u in range(UL):
                b = i * UL + u
                lhs = jnp.concatenate([lt[b, j] for j in range(4)], axis=1)
                rhs = jnp.concatenate([v[k, lcol[j, b]] for j in range(4)], axis=0)
                d = bdot(lhs, rhs)
                base = pl.multiple_of(2 * BLK * b, 2 * BLK)
                pf[pl.ds(base, BLK, stride=2), :] = d[:, :128]
                pf[pl.ds(base + 1, BLK, stride=2), :] = d[:, 128:]
            return 0

        lax.fori_loop(0, NB // UL, body, 0)

    def unpack(slot):
        lane = lax.broadcasted_iota(jnp.int32, (8, 128), 1)

        def body(j, _):
            q = lax.rem(block + 31 - j, 16)
            eight = recv.at[slot, pl.ds(pl.multiple_of(q * 8, 8), 8)]
            pltpu.make_async_copy(eight, eight, rsem.at[slot, q]).wait()
            for u in range(8):
                m = recv[slot, q * 8 + u]
                hi = m[16:24].astype(F32)
                hi0 = jnp.where(lane < 64, hi, 0.0)
                hi1 = pltpu.roll(hi - hi0, 64, 1)
                vr[q, u * 16 : u * 16 + 16, 0:128] = m[0:16]
                vr[q, u * 16 : u * 16 + 16, 128:256] = jnp.concatenate([hi0, hi1], axis=0).astype(BF)
            return 0

        lax.fori_loop(0, 16, body, 0)

    def remote(k):
        def body(i, _):
            ds = []
            for u in range(UR):
                b = i * UR + u
                lhs = jnp.concatenate([rt[b, j] for j in range(2)], axis=1)
                rhs = jnp.concatenate([vr[rslot[j, b]] for j in range(2)], axis=0)
                ds.append(bdot(lhs, rhs))
            for u in range(UR):
                b, d = i * UR + u, ds[u]
                base = pl.multiple_of(2 * BLK * b, 2 * BLK)
                low = 0.9 * (pf[pl.ds(base, BLK, stride=2), :] + d[:, :128])
                high = 0.9 * (pf[pl.ds(base + 1, BLK, stride=2), :] + d[:, 128:])
                p = jnp.concatenate([low, high], axis=1)
                if k + 1 < STEPS:
                    pf[pl.ds(base, BLK, stride=2), :] = low
                    pf[pl.ds(base + 1, BLK, stride=2), :] = high
                    v[k + 1, b] = p.astype(BF)
                else:
                    total = v[0, b].astype(F32) + v[1, b].astype(F32) + v[2, b].astype(F32)
                    v[0, b] = (0.1 * total + p).astype(BF)
            return 0

        lax.fori_loop(0, NB // UR, body, 0)

    def whole_send(slot):
        return pltpu.make_async_copy(
            send.at[slot, pl.ds(0, NDEV - 1)], recv.at[slot, pl.ds(0, NDEV - 1)], ssem.at[slot])

    pl.semaphore_wait(barrier, NDEV - 1)
    for k in range(STEPS):
        slot = k % 2
        if k >= 2:
            whole_send(slot).wait()

        def pack_send(i, first, slot=slot):
            at = [target(i * UP + u) for u in range(first, UP)]
            for u, (t, a, b) in enumerate(at):
                pack(slot, t, u + first)
            for t, a, b in at:
                dispatch(slot, t, a, b)
            return 0

        pack_send(0, 1)
        pack(slot, me, 0)
        own(slot).start()
        lax.fori_loop(1, NDEV // UP, lambda i, _: pack_send(i, 0), 0)
        if k == 0:
            for c in tiles:
                c.wait()
        local(k)
        if k == 0:
            lax.fori_loop(0, F1, forward, 0)
        elif k == 1:
            lax.fori_loop(F1, F2, forward, 0)
        else:
            lax.fori_loop(F2, 16, forward, 0)
        unpack(slot)
        remote(k)
    for slot in (1, 0):
        whole_send(slot).wait()

    nb = BCH // BLK
    scale = float(ROWS * NDEV) ** -0.5
    grad[...] = jnp.zeros_like(grad)

    def delta(c):
        return jnp.concatenate([v[0, c * nb + j] for j in range(nb)], axis=0)

    def add(first, count, bias, d):
        for s in range(count):
            grad[first + s] += d[8 * s : 8 * s + 8]
        grad[NSLAB - 1, pl.ds(bias, 1), :] += d[8 * count : 8 * count + 1]

    def out_grad(c, _):
        cols = pl.ds(pl.multiple_of(c * BCH, BCH), BCH)
        add(0, 32, 0, bdot(hmt[:, cols], delta(c)))
        return 0

    def mid_grad(c, _):
        cols = pl.ds(pl.multiple_of(c * BCH, BCH), BCH)
        dm = (bdot(delta(c), wot[...]) * gm[cols, :].astype(F32)).astype(BF)
        gm[cols, :] = dm
        add(32, 32, 1, bdot(hit[:, cols], dm))
        return 0

    def in_grad(c, _):
        cols = pl.ds(pl.multiple_of(c * BCH, BCH), BCH)
        di = (bdot(gm[cols, :], wmt[...]) * gi[cols, :].astype(F32)).astype(BF)
        gi[cols, :] = di
        add(64, 16, 2, bdot(xt[:, cols], di))
        return 0

    def owner(s):
        return (s * 3) % NDEV

    def scatter(first, count, sem):
        def body(i, _):
            s = first + i
            o = owner(s)

            @pl.when(o != me)
            def _():
                pltpu.make_async_remote_copy(
                    src_ref=grad.at[s], dst_ref=rsr.at[me], send_sem=gsem.at[0], recv_sem=grsem.at[0],
                    device_id=(o // 4, o % 4), device_id_type=MESH,
                ).start()

            @pl.when(o == me)
            def _():
                pltpu.make_async_copy(grad.at[s], rsr.at[me], grsem.at[0]).start()

            return 0

        lax.fori_loop(0, count, body, 0)

    lax.fori_loop(0, ROWS // BCH, out_grad, 0)
    scatter(0, 32, 0)
    lax.fori_loop(0, ROWS // BCH, mid_grad, 0)
    scatter(32, 32, 0)
    lax.fori_loop(0, ROWS // BCH, in_grad, 0)
    scatter(64, 17, 0)

    out_di = pltpu.make_async_copy(gi, o_di, osem)
    out_di.start()

    inverse = (me * 43) % NDEV
    mine = inverse < NSLAB

    @pl.when(mine)
    def _():
        pltpu.make_async_copy(rsr, rsr, grsem.at[0]).wait()

        def body(i, acc):
            part = [rsr[i * 8 + j] for j in range(8)]
            while len(part) > 1:
                part = [part[j] + part[j + 1] for j in range(0, len(part), 2)]
            return acc + part[0]

        total = lax.fori_loop(0, NDEV // 8, body, jnp.zeros((8, 256), F32))
        total = scale * total
        gall[inverse] = jnp.concatenate([total[:, :128], total[:, 128:]], axis=0).astype(BF)

        def spread(i, _):
            _, a, b = target(i)
            pltpu.make_async_remote_copy(
                src_ref=gall.at[inverse], dst_ref=gall.at[inverse], send_sem=asem.at[0], recv_sem=arsem.at[0],
                device_id=(a, b), device_id_type=MESH,
            ).start()
            return 0

        lax.fori_loop(1, NDEV, spread, 0)
        pltpu.make_async_copy(gall.at[pl.ds(0, NSLAB - 1)], gall.at[pl.ds(0, NSLAB - 1)], arsem.at[0]).wait()
        pltpu.make_async_copy(recv.at[0, pl.ds(0, NDEV - 1), pl.ds(0, 16)], recv.at[0, pl.ds(0, NDEV - 1), pl.ds(0, 16)], asem.at[0]).wait()
        pltpu.make_async_copy(grad.at[pl.ds(0, NSLAB - 1)], grad.at[pl.ds(0, NSLAB - 1)], gsem.at[0]).wait()

    @pl.when(jnp.logical_not(mine))
    def _():
        pltpu.make_async_copy(gall, gall, arsem.at[0]).wait()
        pltpu.make_async_copy(grad, grad, gsem.at[0]).wait()

    o_grad[...] = gall[...]
    out_di.wait()


def finish(grad, di, w_in, o_win, o_bin, o_wmid, o_bmid, o_wout, o_bout, o_fg):
    o_fg[...] = lax.dot_general(di[...], w_in[...], (((1,), (1,)), ((), ())), preferred_element_type=F32)

    def slabs(first, count):
        parts = [grad[s].astype(F32) for s in range(first, first + count)]
        low = jnp.concatenate([p[0:8] for p in parts], axis=0)
        high = jnp.concatenate([p[8:16] for p in parts], axis=0)
        return jnp.concatenate([low, high], axis=1)

    @pl.when(pl.program_id(0) == 0)
    def _():
        o_wout[...] = slabs(0, 32).T[0:172]
        o_wmid[...] = slabs(32, 32)
        o_win[...] = slabs(64, 16)
        bias = slabs(NSLAB - 1, 1)
        o_bout[...] = bias[0:1, 0:172]
        o_bmid[...] = bias[1:2]
        o_bin[...] = bias[2:3]


def shards(
    features, weight_in, bias_in, weight_mid, bias_mid, weight_out, cotangent,
    local_tiles, local_columns, remote_tiles, remote_slots, send_rows,
):
    any_ = pl.BlockSpec(memory_space=pl.ANY)
    smem = pl.BlockSpec(memory_space=pltpu.SMEM)
    vmem = pl.BlockSpec(memory_space=pltpu.VMEM)
    dma = pltpu.SemaphoreType.DMA
    grad, di = pl.pallas_call(
        kernel,
        out_shape=[jax.ShapeDtypeStruct((NSLAB, 16, 128), BF), jax.ShapeDtypeStruct((ROWS, 256), BF)],
        in_specs=[any_] * 8 + [smem, any_, smem, smem],
        out_specs=[vmem, any_],
        scratch_shapes=[
            pltpu.VMEM((NB, 4, BLK, BLK), BF),
            pltpu.VMEM((NB, 2, BLK, BLK), BF),
            pltpu.VMEM((3, NB, BLK, 256), BF),
            pltpu.VMEM((2 * ROWS, 128), F32),
            pltpu.VMEM((UP, 32, 128), F32),
            pltpu.VMEM((2, NDEV, 24, 128), BF),
            pltpu.VMEM((2, NDEV, 24, 128), BF),
            pltpu.VMEM((16, BLK, 256), BF),
            pltpu.VMEM((4, 172, CH), F32),
            pltpu.VMEM((2, FCH, 128), BF),
            pltpu.VMEM((272, ROWS), BF),
            pltpu.VMEM((272, ROWS), BF),
            pltpu.VMEM((144, ROWS), BF),
            pltpu.VMEM((ROWS, 256), BF),
            pltpu.VMEM((ROWS, 256), BF),
            pltpu.VMEM((128, 256), BF),
            pltpu.VMEM((1, 256), F32),
            pltpu.VMEM((256, 256), BF),
            pltpu.VMEM((1, 256), F32),
            pltpu.VMEM((172, 256), BF),
            pltpu.VMEM((256, 256), BF),
            pltpu.VMEM((256, 256), BF),
            pltpu.VMEM((NSLAB, 8, 256), F32),
            pltpu.VMEM((NDEV, 8, 256), F32),
            pltpu.VMEM((NSLAB, 16, 128), BF),
            dma((4,)), dma((2,)), dma((2,)), dma((5,)), dma((2,)), dma((2, 16)),
            dma((1,)), dma((1,)), dma((1,)), dma((1,)), dma,
        ],
        compiler_params=pltpu.CompilerParams(
            collective_id=0, has_side_effects=True, vmem_limit_bytes=63 * 2**20
        ),
        cost_estimate=pl.CostEstimate(flops=13 * 10**9, bytes_accessed=30 * 10**6, transcendentals=4 * 10**6),
        name="appnp_backward",
    )(
        features, weight_in, bias_in.reshape(1, 256), weight_mid, bias_mid.reshape(1, 256), weight_out.T, cotangent.T,
        local_tiles, local_columns.T, remote_tiles, remote_slots.T, send_rows.transpose(0, 2, 1),
    )
    fch = 4096
    win, bi, wmid, bm, wout, bo, fg = pl.pallas_call(
        finish,
        grid=(ROWS // fch,),
        out_shape=[
            jax.ShapeDtypeStruct(s, F32)
            for s in ((128, 256), (1, 256), (256, 256), (1, 256), (172, 256), (1, 172), (ROWS, 128))
        ],
        in_specs=[vmem, pl.BlockSpec((fch, 256), lambda i: (i, 0)), vmem],
        out_specs=[vmem] * 6 + [pl.BlockSpec((fch, 128), lambda i: (i, 0))],
        name="finish",
    )(grad, di, weight_in)
    return win, bi.reshape(256), wmid, bm.reshape(256), wout.T, bo.reshape(172), fg


def solution(mesh):
    both = ("dp", "sub")
    return jax.shard_map(
        shards,
        mesh=mesh,
        in_specs=(
            P(both, None), P(), P(), P(), P(), P(), P(both, None), P(both, None, None, None),
            P(both, None), P(both, None, None, None), P(both, None), P(both, None, None),
        ),
        out_specs=(P(), P(), P(), P(), P(), P(), P(both, None)),
        check_vma=False,
    )
```
